512 devices in a mesh: sec: 64 (over x, z, core), term: 8 (over y).
Axes of the slice: x: 4, y: 8, z: 8, core: 2. Of those that a mesh axis runs over, the one named last changes fastest.
Arguments:
- wavefunction: bfloat16 [3, 16384, 256], P(None, 'sec'), may hold values from -6 to 6
- left_blocks: bfloat16 [128, 64, 256, 256], P('term', 'sec'), may hold values from -0.03125 to 0.03125
- right_blocks: bfloat16 [128, 64, 256, 256], P('term', 'sec'), may hold values from -0.375 to 0.375
- term_shift: int32 [128], P('term'), may hold values from -2 to 2, as said below
- left_sizes: int32 [64], replicated, may hold values from 64 to 256, as said below
- right_sizes: int32 [64], replicated, may hold values from 64 to 256, as said below
Outputs:
- sigma: bfloat16 [3, 16384, 256], P(None, ('sec', 'term'))
The draws below stay inside these ranges and needn't reach their ends.
Inputs may be any that keep to these rules, and one draw needn't show every extreme that they name: `term_shift`: every offset from -2 to 2 is taken by some term. `left_sizes`: valid states of each left sector; rows beyond them in its 256 are padding; some sector has all 256. `right_sizes`: valid states of each right sector; columns beyond them in its 256 are padding; some sector has all 256.
All inputs are finite; a program needn't handle non-finite values.
Results may differ from the reference program's by a relative error of at most 0.0049.
Values may be sent and summed in bfloat16 or wider, within the bound.
A program may use at most 64 MiB of HBM per device.

```python
import jax
import jax.numpy as jnp
from jax import lax

BL = 256
BR = 256
VECS = 3
SECTORS = 64
TERMS = 128


def sector_sizes(key, count, largest):
    first, second = jax.random.split(key)
    values = jax.random.randint(first, (count,), largest // 4, largest + 1)
    where = jax.random.randint(second, (), 0, count)
    return jnp.where(jnp.arange(count) == where, largest, values).astype(jnp.int32)


def draw_left_sizes(key, part):
    key = jax.random.fold_in(key, 11)
    return sector_sizes(key, SECTORS, BL)


def draw_right_sizes(key, part):
    key = jax.random.fold_in(key, 23)
    return sector_sizes(key, SECTORS, BR)


def draw_term_shift(key, part):
    key = jax.random.fold_in(key, 37)
    order = jax.random.permutation(key, TERMS)
    return (order % 5 - 2).astype(jnp.int32)


def block_levels(rng, shape, cuts, least, high):
    loudness, own = 1.0, jax.random.fold_in(rng, 6)
    for axis_at, parts in cuts:
        draws = jnp.exp(jax.random.uniform(jax.random.fold_in(own, axis_at), (parts,), jnp.float32, least / len(cuts), high / len(cuts)))
        loudness = loudness * jnp.repeat(draws, shape[axis_at] // parts).reshape([-1 if axis == axis_at else 1 for axis in range(len(shape))])
    return loudness


def normal_values(stream_key, dims, deviation, reach, cuts=(), dtype=jnp.bfloat16):
    values = jax.random.normal(stream_key, dims, jnp.float32) * deviation
    if len(cuts) > 0:
        values = block_levels(stream_key, dims, cuts, -0.22, 0.18) * values
    return jnp.clip(values, min=-reach, max=reach).astype(dtype)


def setup_inputs(seed: int = 0) -> dict:
    seeds = jax.random.split(jax.random.key(seed), 7)
    return {
        "wavefunction": normal_values(seeds[0], (VECS, SECTORS * BL, BR), 1.0, 6.0, ((1, 64),)),
        "left_blocks": normal_values(seeds[1], (TERMS, SECTORS, BL, BL), (BL * TERMS) ** -0.5, 0.03125, ((0, 8), (1, 64))),
        "right_blocks": normal_values(seeds[2], (TERMS, SECTORS, BR, BR), BR ** -0.5, 0.375, ((0, 8), (1, 64))),
        "term_shift": draw_term_shift(jax.random.fold_in(seeds[6], 71), 0),
        "left_sizes": draw_left_sizes(jax.random.fold_in(seeds[6], 71), 0),
        "right_sizes": draw_right_sizes(jax.random.fold_in(seeds[6], 71), 0),
    }


def valid_cells(left_sizes, right_sizes):
    row_ok = jnp.arange(BL)[None, :] < left_sizes[:, None]
    col_ok = jnp.arange(BR)[None, :] < right_sizes[:, None]
    return row_ok[:, :, None] & col_ok[:, None, :]


def reference(wavefunction, left_blocks, right_blocks, term_shift, left_sizes, right_sizes):
    valid = valid_cells(left_sizes, right_sizes)
    blocks = wavefunction.reshape(VECS, SECTORS, BL, BR) * valid.astype(jnp.bfloat16)[None]
    padded = jnp.pad(blocks.astype(jnp.float32), ((0, 0), (2, 2), (0, 0), (0, 0)))

    def one_term(running, operands):
        left_one, right_one, offset = operands
        start = (offset + 2).astype(jnp.int32)
        source = lax.dynamic_slice_in_dim(padded, start, SECTORS, 1)
        product = jnp.einsum("sab,vsbc->vsac", left_one.astype(jnp.float32), source)
        product = product.astype(jnp.bfloat16)
        product = lax.optimization_barrier(product)
        product = product.astype(jnp.float32)
        return running + jnp.einsum("vsac,sdc->vsad", product, right_one.astype(jnp.float32)), None

    start_total = jnp.zeros((VECS, SECTORS, BL, BR), jnp.float32)
    total, _ = lax.scan(one_term, start_total, (left_blocks, right_blocks, term_shift))
    result = total * valid.astype(jnp.float32)[None]
    return result.reshape(VECS, SECTORS * BL, BR).astype(jnp.bfloat16)
```

```python
import jax
import jax.numpy as jnp
from jax import lax
from jax.experimental import pallas as pl
from jax.experimental.pallas import tpu as pltpu
from jax.sharding import PartitionSpec as P

MESH = pl.DeviceIdType.MESH
F32, BF16 = jnp.float32, jnp.bfloat16
ROWS_BY_ROWS = (((1,), (1,)), ((), ()))
PEERS = (4, 3, 5, 2, 6, 1, 7)


def kernel(
    sectors, groups,
    wave_hbm, left_hbm, right_hbm, shift_hbm, lsize_hbm, rsize_hbm,
    out_ref,
    wave, src0, src1, src2, left, right, prod, total, part, landed, shift, lsize, rsize,
    load_sem, z_send, z_recv, c_send, c_recv, f_send, f_recv, y_send, y_recv,
):
    vecs, rows, cols = wave.shape
    terms = left.shape[0]
    piece = rows // groups
    src = (src0, src1, src2)
    s = lax.axis_index("sec")
    t = lax.axis_index("term")
    core = lax.rem(s, 2)
    twin = s + 1 - 2 * core
    up = lax.rem(s + 2, sectors)
    down = lax.rem(s + sectors - 2, sectors)

    def peer(d):
        return lax.rem(t + d, groups)

    barrier = pltpu.get_barrier_semaphore()
    for place in ((twin, t), (up, t), (down, t), *((s, peer(d)) for d in PEERS)):
        pl.semaphore_signal(barrier, inc=1, device_id=place, device_id_type=MESH)

    loads = [
        pltpu.make_async_copy(lsize_hbm, lsize, load_sem.at[0]),
        pltpu.make_async_copy(rsize_hbm, rsize, load_sem.at[1]),
        pltpu.make_async_copy(wave_hbm, wave, load_sem.at[2]),
        pltpu.make_async_copy(shift_hbm, shift, load_sem.at[3]),
        pltpu.make_async_copy(left_hbm.at[:, 0], left, load_sem.at[4]),
    ]
    loads += [
        pltpu.make_async_copy(right_hbm.at[k, 0], right.at[:, pl.ds(k * cols, cols)], load_sem.at[5 + k])
        for k in range(terms)
    ]
    for load in loads:
        load.start()

    for v in range(vecs):
        src[v][5] = jnp.zeros((rows, cols), BF16)
    loads[0].wait()
    loads[1].wait()
    row_at = lax.broadcasted_iota(jnp.int32, (rows, cols), 0)
    col_at = lax.broadcasted_iota(jnp.int32, (rows, cols), 1)
    valid = jnp.where((row_at < lsize[s]) & (col_at < rsize[s]), 1.0, 0.0).astype(F32)
    loads[2].wait()
    for v in range(vecs):
        src[v][2] = wave[v] * valid.astype(BF16)
    pl.semaphore_wait(barrier, 3 + len(PEERS))

    up_from = jnp.where(s + 2 >= sectors, 5, 2)
    down_from = jnp.where(s < 2, 5, 2)
    first_to = jnp.where(core == 1, up, down)
    first_from = jnp.where(core == 1, up_from, down_from)
    first_slot = 4 * (1 - core)
    second_to = jnp.where(core == 1, down, up)
    second_from = jnp.where(core == 1, down_from, up_from)
    second_slot = 4 * core

    def first(v):
        return pltpu.make_async_remote_copy(
            src_ref=src[v].at[first_from], dst_ref=src[v].at[first_slot], send_sem=z_send.at[0, v], recv_sem=z_recv.at[0, v],
            device_id=(first_to, t), device_id_type=MESH)

    def second(v):
        return pltpu.make_async_remote_copy(
            src_ref=src[v].at[second_from], dst_ref=src[v].at[second_slot], send_sem=z_send.at[1, v], recv_sem=z_recv.at[1, v],
            device_id=(second_to, t), device_id_type=MESH)

    def own(v):
        return pltpu.make_async_remote_copy(
            src_ref=src[v].at[2], dst_ref=src[v].at[1 + 2 * core], send_sem=c_send.at[v], recv_sem=c_recv.at[v],
            device_id=(twin, t), device_id_type=MESH)

    def onward(v):
        return pltpu.make_async_remote_copy(
            src_ref=src[v].at[first_slot], dst_ref=src[v].at[3 - 2 * core], send_sem=f_send.at[v], recv_sem=f_recv.at[v],
            device_id=(twin, t), device_id_type=MESH)

    def share(v, d):
        there = pl.multiple_of(peer(d) * piece, piece)
        return pltpu.make_async_remote_copy(
            src_ref=part.at[v, pl.ds(there, piece)], dst_ref=landed.at[v, d - 1], send_sem=y_send.at[v, d - 1], recv_sem=y_recv.at[v, d - 1],
            device_id=(s, peer(d)), device_id_type=MESH)

    for v in range(vecs):
        first(v).start()
        second(v).start()
    for v in range(vecs):
        own(v).start()
    for load in loads[3:]:
        load.wait()

    for v in range(vecs):
        first(v).wait_recv()
        onward(v).start()
        own(v).wait_recv()
        second(v).wait_recv()
        onward(v).wait_recv()
        for k in range(terms):
            prod[:, k * cols:(k + 1) * cols] = jnp.dot(
                left[k], src[v][shift[k] + 2], preferred_element_type=F32
            ).astype(BF16)
        summed = lax.dot_general(prod[...], right[...], ROWS_BY_ROWS, preferred_element_type=F32) * valid
        total[v] = summed
        part[v] = summed.astype(BF16)
        for d in PEERS:
            share(v, d).start()

    mine = pl.multiple_of(t * piece, piece)
    for v in range(vecs):
        result = total[v, pl.ds(mine, piece)]
        for d in PEERS[::-1]:
            share(v, d).wait_recv()
            result = result + landed[v, d - 1].astype(F32)
        out_ref[v] = result.astype(BF16)
    for v in range(vecs):
        first(v).wait_send()
        second(v).wait_send()
        own(v).wait_send()
        onward(v).wait_send()
        for d in PEERS:
            share(v, d).wait_send()


def solution(mesh):
    sectors, groups = mesh.shape["sec"], mesh.shape["term"]

    def per_device(wave, left, right, shift, lsize, rsize):
        vecs, rows, cols = wave.shape
        terms = left.shape[0]
        piece = rows // groups
        far = len(PEERS)

        def body(*refs):
            kernel(sectors, groups, *refs)

        dma = pltpu.SemaphoreType.DMA
        return pl.pallas_call(
            body,
            name="sigma",
            out_shape=jax.ShapeDtypeStruct((vecs, piece, cols), BF16),
            in_specs=[pl.BlockSpec(memory_space=pltpu.HBM)] * 6,
            out_specs=pl.BlockSpec(memory_space=pltpu.VMEM),
            scratch_shapes=[
                pltpu.VMEM((vecs, rows, cols), BF16),
                *[pltpu.VMEM((6, rows, cols), BF16) for _ in range(vecs)],
                pltpu.VMEM((terms, rows, rows), BF16),
                pltpu.VMEM((cols, terms * cols), BF16),
                pltpu.VMEM((rows, terms * cols), BF16),
                pltpu.VMEM((vecs, rows, cols), F32),
                pltpu.VMEM((vecs, rows, cols), BF16),
                pltpu.VMEM((vecs, far, piece, cols), BF16),
                pltpu.SMEM(shift.shape, jnp.int32),
                pltpu.SMEM(lsize.shape, jnp.int32),
                pltpu.SMEM(rsize.shape, jnp.int32),
                dma((5 + terms,)),
                dma((2, vecs)), dma((2, vecs)),
                dma((vecs,)), dma((vecs,)),
                dma((vecs,)), dma((vecs,)),
                dma((vecs, far)), dma((vecs, far)),
            ],
            compiler_params=pltpu.CompilerParams(
                collective_id=0, has_side_effects=True, vmem_limit_bytes=60 * 2**20
            ),
        )(wave, left, right, shift, lsize, rsize)

    return jax.shard_map(
        per_device,
        mesh=mesh,
        in_specs=(P(None, "sec", None), P("term", "sec", None, None), P("term", "sec", None, None), P("term"), P(), P()),
        out_specs=P(None, ("sec", "term"), None),
        check_vma=False,
    )
```

```python
import jax
import jax.numpy as jnp
from jax import lax
from jax.experimental import pallas as pl
from jax.experimental.pallas import tpu as pltpu
from jax.sharding import PartitionSpec as P

MESH = pl.DeviceIdType.MESH
F32, BF16 = jnp.float32, jnp.bfloat16
ROWS_BY_ROWS = (((1,), (1,)), ((), ()))
LINE = 8
PEERS = (4, 3, 5, 2, 6, 1, 7)


def kernel(
    sectors, groups,
    wave_hbm, left_hbm, right_hbm, shift_hbm, lsize_hbm, rsize_hbm,
    out_ref,
    src0, src1, src2, left, right, prod, masked, mask, total, part, landed, shift, lsize, rsize,
    load_sem, z_send, z_recv, c_send, c_recv, f_send, f_recv, y_send, y_recv, told,
):
    vecs, rows, cols = total.shape
    terms = left.shape[0]
    piece = rows // groups
    src = (src0, src1, src2)
    s = lax.axis_index("sec")
    t = lax.axis_index("term")
    core = lax.rem(s, 2)
    twin = s + 1 - 2 * core
    up = lax.rem(s + 2, sectors)
    down = lax.rem(s + sectors - 2, sectors)

    def peer(d):
        return lax.rem(t + d, groups)

    barrier = pltpu.get_barrier_semaphore()
    def greet(sem, place):
        pl.semaphore_signal(sem, inc=1, device_id=place, device_id_type=MESH)

    at = lax.rem(s // 2, LINE)
    last, before = at == LINE - 1, at == LINE - 2
    for place in ((twin, t), (up, t), (down, t)):
        greet(barrier, place)

    @pl.when(jnp.logical_not(last))
    def _():
        for d in PEERS:
            greet(barrier, (s, peer(d)))

    first_to = jnp.where(core == 1, up, down)
    first_slot = 4 * (1 - core)
    second_to = jnp.where(core == 1, down, up)
    second_slot = 4 * core
    own_slot = 1 + 2 * core
    onward_slot = 3 - 2 * core

    def first(v):
        return pltpu.make_async_remote_copy(
            src_ref=wave_hbm.at[v], dst_ref=src[v].at[first_slot], send_sem=z_send.at[0, v], recv_sem=z_recv.at[0, v],
            device_id=(first_to, t), device_id_type=MESH)

    def second(v):
        return pltpu.make_async_remote_copy(
            src_ref=wave_hbm.at[v], dst_ref=src[v].at[second_slot], send_sem=z_send.at[1, v], recv_sem=z_recv.at[1, v],
            device_id=(second_to, t), device_id_type=MESH)

    def own(v):
        return pltpu.make_async_remote_copy(
            src_ref=wave_hbm.at[v], dst_ref=src[v].at[own_slot], send_sem=c_send.at[v], recv_sem=c_recv.at[v],
            device_id=(twin, t), device_id_type=MESH)

    def onward(v):
        return pltpu.make_async_remote_copy(
            src_ref=src[v].at[first_slot], dst_ref=src[v].at[onward_slot], send_sem=f_send.at[v], recv_sem=f_recv.at[v],
            device_id=(twin, t), device_id_type=MESH)

    def share(v, d):
        there = pl.multiple_of(peer(d) * piece, piece)
        return pltpu.make_async_remote_copy(
            src_ref=part.at[v, pl.ds(there, piece)], dst_ref=landed.at[v, d - 1], send_sem=y_send.at[v, d - 1], recv_sem=y_recv.at[v, d - 1],
            device_id=(s, peer(d)), device_id_type=MESH)

    @pl.when(last)
    def _():
        pl.semaphore_wait(barrier, 3)

    @pl.when(jnp.logical_not(last))
    def _():
        pl.semaphore_wait(barrier, 3 + len(PEERS))

    for v in range(vecs):
        first(v).start()
        second(v).start()
    for v in range(vecs):
        own(v).start()

    loads = [
        pltpu.make_async_copy(lsize_hbm, lsize, load_sem.at[0]),
        pltpu.make_async_copy(rsize_hbm, rsize, load_sem.at[1]),
        pltpu.make_async_copy(shift_hbm, shift, load_sem.at[2]),
        pltpu.make_async_copy(left_hbm.at[:, 0], left, load_sem.at[3]),
    ]
    loads += [pltpu.make_async_copy(wave_hbm.at[v], src[v].at[2], load_sem.at[4 + v]) for v in range(vecs)]
    loads += [
        pltpu.make_async_copy(right_hbm.at[k, 0], right.at[:, pl.ds(k * cols, cols)], load_sem.at[4 + vecs + k])
        for k in range(terms)
    ]
    for load in loads:
        load.start()

    loads[0].wait()
    loads[1].wait()
    row_at = lax.broadcasted_iota(jnp.int32, (rows, cols), 0)
    col_at = lax.broadcasted_iota(jnp.int32, (rows, cols), 1)
    for o in range(5):
        q = s + o - 2
        inside = (q >= 0) & (q < sectors)
        q = jnp.clip(q, 0, sectors - 1)
        limit = jnp.where(inside, lsize[q], 0)
        mask[o] = jnp.where((row_at < limit) & (col_at < rsize[q]), 1.0, 0.0).astype(BF16)
    for load in loads[2:]:
        load.wait()

    @pl.when(before)
    def _():
        for d in PEERS:
            greet(told, (s, peer(d)))
        pl.semaphore_wait(told, len(PEERS))
        greet(told, (up, t))

    def admit(v, slot):
        masked[slot] = src[v][slot] * mask[slot]

    for v in range(vecs):
        admit(v, 2)
        first(v).wait_recv()
        onward(v).start()
        own(v).wait_recv()
        admit(v, onward_slot)
        admit(v, first_slot)
        second(v).wait_recv()
        admit(v, second_slot)
        onward(v).wait_recv()
        admit(v, own_slot)
        for k in range(terms):
            prod[:, k * cols:(k + 1) * cols] = jnp.dot(
                left[k], masked[shift[k] + 2], preferred_element_type=F32
            ).astype(BF16)
        summed = lax.dot_general(prod[...], right[...], ROWS_BY_ROWS, preferred_element_type=F32) * mask[2].astype(F32)
        total[v] = summed
        part[v] = summed.astype(BF16)
        if v == 0:
            @pl.when(last)
            def _():
                pl.semaphore_wait(told, 1)

        for d in PEERS:
            share(v, d).start()

    for v in range(vecs):
        first(v).wait_send()
        second(v).wait_send()
        own(v).wait_send()
        onward(v).wait_send()
        for d in PEERS:
            share(v, d).wait_send()
    for v in range(vecs):
        result = total[v, pl.ds(pl.multiple_of(t * piece, piece), piece)]
        for d in PEERS[::-1]:
            share(v, d).wait_recv()
            result = result + landed[v, d - 1].astype(F32)
        out_ref[v] = result.astype(BF16)


def solution(mesh):
    sectors, groups = mesh.shape["sec"], mesh.shape["term"]

    def per_device(wave, left, right, shift, lsize, rsize):
        vecs, rows, cols = wave.shape
        terms = left.shape[0]
        piece = rows // groups
        far = len(PEERS)

        def body(*refs):
            kernel(sectors, groups, *refs)

        dma = pltpu.SemaphoreType.DMA
        return pl.pallas_call(
            body,
            name="sigma",
            out_shape=jax.ShapeDtypeStruct((vecs, piece, cols), BF16),
            in_specs=[pl.BlockSpec(memory_space=pltpu.HBM)] * 6,
            out_specs=pl.BlockSpec(memory_space=pltpu.VMEM),
            scratch_shapes=[
                *[pltpu.VMEM((5, rows, cols), BF16) for _ in range(vecs)],
                pltpu.VMEM((terms, rows, rows), BF16),
                pltpu.VMEM((cols, terms * cols), BF16),
                pltpu.VMEM((rows, terms * cols), BF16),
                pltpu.VMEM((5, rows, cols), BF16),
                pltpu.VMEM((5, rows, cols), BF16),
                pltpu.VMEM((vecs, rows, cols), F32),
                pltpu.VMEM((vecs, rows, cols), BF16),
                pltpu.VMEM((vecs, far, piece, cols), BF16),
                pltpu.SMEM(shift.shape, jnp.int32),
                pltpu.SMEM(lsize.shape, jnp.int32),
                pltpu.SMEM(rsize.shape, jnp.int32),
                dma((4 + vecs + terms,)),
                dma((2, vecs)), dma((2, vecs)),
                dma((vecs,)), dma((vecs,)),
                dma((vecs,)), dma((vecs,)),
                dma((vecs, far)), dma((vecs, far)),
                pltpu.SemaphoreType.REGULAR,
            ],
            compiler_params=pltpu.CompilerParams(
                collective_id=0, has_side_effects=True, vmem_limit_bytes=60 * 2**20
            ),
        )(wave, left, right, shift, lsize, rsize)

    return jax.shard_map(
        per_device,
        mesh=mesh,
        in_specs=(P(None, "sec", None), P("term", "sec", None, None), P("term", "sec", None, None), P("term"), P(), P()),
        out_specs=P(None, ("sec", "term"), None),
        check_vma=False,
    )
```

```python
import jax
import jax.numpy as jnp
from jax import lax
from jax.experimental import pallas as pl
from jax.experimental.pallas import tpu as pltpu
from jax.sharding import PartitionSpec as P

MESH = pl.DeviceIdType.MESH
F32, BF16 = jnp.float32, jnp.bfloat16
ROWS_BY_ROWS = (((1,), (1,)), ((), ()))
LINE = 8
PEERS = (4, 3, 5, 2, 6, 1, 7)


def kernel(
    sectors, groups,
    wave_hbm, left_hbm, right_hbm, shift_hbm, lsize_hbm, rsize_hbm,
    out_ref,
    src0, src1, src2, left, right, prod, masked, mask, total, part, landed, shift, lsize, rsize,
    load_sem, z_send, z_recv, c_send, c_recv, f_send, f_recv, y_send, y_recv, told, near,
):
    vecs, rows, cols = total.shape
    terms = left.shape[0]
    piece = rows // groups
    src = (src0, src1, src2)
    s = lax.axis_index("sec")
    t = lax.axis_index("term")
    core = lax.rem(s, 2)
    twin = s + 1 - 2 * core
    up, down = s + 2, s - 2
    has_up, has_down = up < sectors, down >= 0
    beside = s + 2 * core - 1
    along = has_up.astype(jnp.int32) + has_down.astype(jnp.int32) + jnp.where(core == 1, has_up, has_down).astype(jnp.int32)

    def peer(d):
        return lax.rem(t + d, groups)

    barrier = pltpu.get_barrier_semaphore()
    def greet(sem, place):
        pl.semaphore_signal(sem, inc=1, device_id=place, device_id_type=MESH)

    at = lax.rem(s // 2, LINE)
    last, before = at == LINE - 1, at == LINE - 2
    after = (at == 0) & has_down
    pl.when(jnp.logical_not(last))(lambda: greet(barrier, (twin, t)))

    @pl.when(has_up & jnp.logical_not(last | before))
    def _():
        greet(barrier, (up, t))

    @pl.when(has_down)
    def _():
        greet(barrier, (down, t))

    first_up = core == 1
    first_goes = jnp.where(first_up, has_up, has_down)

    @pl.when(first_goes & jnp.logical_not((last | before) & first_up))
    def _():
        greet(barrier, (beside, t))

    @pl.when(jnp.logical_not(last))
    def _():
        for d in PEERS:
            greet(barrier, (s, peer(d)))

    first_to = jnp.where(core == 1, up, down)
    first_slot = 4 * (1 - core)
    second_to = jnp.where(core == 1, down, up)
    second_slot = 4 * core
    own_slot = 1 + 2 * core
    onward_slot = 3 - 2 * core
    second_goes = jnp.where(core == 1, has_down, has_up)
    first_comes, second_comes = second_goes, first_goes

    def first(v):
        return pltpu.make_async_remote_copy(
            src_ref=wave_hbm.at[v], dst_ref=src[v].at[first_slot], send_sem=z_send.at[0, v], recv_sem=z_recv.at[0, v],
            device_id=(first_to, t), device_id_type=MESH)

    def second(v):
        return pltpu.make_async_remote_copy(
            src_ref=wave_hbm.at[v], dst_ref=src[v].at[second_slot], send_sem=z_send.at[1, v], recv_sem=z_recv.at[1, v],
            device_id=(second_to, t), device_id_type=MESH)

    def own(v):
        return pltpu.make_async_remote_copy(
            src_ref=wave_hbm.at[v], dst_ref=src[v].at[own_slot], send_sem=c_send.at[v], recv_sem=c_recv.at[v],
            device_id=(twin, t), device_id_type=MESH)

    def onward(v):
        return pltpu.make_async_remote_copy(
            src_ref=src[v].at[first_slot], dst_ref=src[v].at[onward_slot], send_sem=f_send.at[v], recv_sem=f_recv.at[v],
            device_id=(twin, t), device_id_type=MESH)

    def relay():
        v = vecs - 1
        return pltpu.make_async_remote_copy(
            src_ref=src[v].at[onward_slot], dst_ref=src[v].at[first_slot], send_sem=z_send.at[1, v], recv_sem=z_recv.at[1, v],
            device_id=(beside, t), device_id_type=MESH)

    def share(v, d):
        there = pl.multiple_of(peer(d) * piece, piece)
        return pltpu.make_async_remote_copy(
            src_ref=part.at[v, pl.ds(there, piece)], dst_ref=landed.at[v, d - 1], send_sem=y_send.at[v, d - 1], recv_sem=y_recv.at[v, d - 1],
            device_id=(s, peer(d)), device_id_type=MESH)

    @pl.when(last)
    def _():
        @pl.when(has_up)
        def _():
            pl.semaphore_wait(barrier, 1 + core)

        @pl.when(has_up)
        def _():
            greet(told, (up, t))

        @pl.when(has_up & first_up)
        def _():
            greet(told, (beside, t))

    @pl.when(jnp.logical_not(last))
    def _():
        pl.semaphore_wait(barrier, 1 + along - jnp.where(after, 2 - core, 0) + len(PEERS))

    for v in range(vecs):
        pl.when(first_goes & jnp.logical_not((after | last) & (core == 0)))(first(v).start)
        if v < vecs - 1:
            pl.when(second_goes & jnp.logical_not((after | last) & (core == 1)))(second(v).start)

    @pl.when(before)
    def _():
        greet(near, (up, t))
        pl.when(core == 1)(lambda: greet(near, (beside, t)))

    @pl.when(last)
    def _():
        pl.semaphore_wait(near, 2 - core)

    for v in range(vecs):
        pl.when(last & (core == 0))(first(v).start)
        if v < vecs - 1:
            pl.when(last & (core == 1))(second(v).start)
    for v in range(vecs - 1, -1, -1):
        own(v).start()

    own(vecs - 1).wait_recv()
    pl.when(first_goes & jnp.logical_not(after & (core == 0)))(relay().start)

    loads = [
        pltpu.make_async_copy(lsize_hbm, lsize, load_sem.at[0]),
        pltpu.make_async_copy(rsize_hbm, rsize, load_sem.at[1]),
        pltpu.make_async_copy(shift_hbm, shift, load_sem.at[2]),
        pltpu.make_async_copy(left_hbm.at[:, 0], left, load_sem.at[3]),
    ]
    loads += [pltpu.make_async_copy(wave_hbm.at[v], src[v].at[2], load_sem.at[4 + v]) for v in range(vecs)]
    loads += [
        pltpu.make_async_copy(right_hbm.at[k, 0], right.at[:, pl.ds(k * cols, cols)], load_sem.at[4 + vecs + k])
        for k in range(terms)
    ]
    for load in loads:
        load.start()

    loads[0].wait()
    loads[1].wait()
    row_at = lax.broadcasted_iota(jnp.int32, (rows, cols), 0)
    col_at = lax.broadcasted_iota(jnp.int32, (rows, cols), 1)
    for o in range(5):
        q = s + o - 2
        inside = (q >= 0) & (q < sectors)
        q = jnp.clip(q, 0, sectors - 1)
        limit = jnp.where(inside, lsize[q], 0)
        mask[o] = jnp.where((row_at < limit) & (col_at < rsize[q]), 1.0, 0.0).astype(BF16)
    for load in loads[2:]:
        load.wait()

    @pl.when(after)
    def _():
        pl.semaphore_wait(told, 2 - core)

    for v in range(vecs):
        pl.when(after & (core == 0))(first(v).start)
        if v < vecs - 1:
            pl.when(after & (core == 1))(second(v).start)
    pl.when(after & (core == 0))(relay().start)

    @pl.when(before)
    def _():
        for d in PEERS:
            greet(told, (s, peer(d)))
        pl.semaphore_wait(told, len(PEERS))
        greet(told, (up, t))

    def admit(v, slot):
        masked[slot] = src[v][slot] * mask[slot]

    @pl.when(jnp.logical_not(first_comes))
    def _():
        masked[first_slot] = jnp.zeros((rows, cols), BF16)

    @pl.when(jnp.logical_not(second_comes))
    def _():
        masked[second_slot] = jnp.zeros((rows, cols), BF16)
        masked[own_slot] = jnp.zeros((rows, cols), BF16)

    for v in range(vecs):
        admit(v, 2)
        @pl.when(first_comes)
        def _():
            first(v).wait_recv()
            onward(v).start()

        if v < vecs - 1:
            own(v).wait_recv()
        admit(v, onward_slot)

        @pl.when(first_comes)
        def _():
            admit(v, first_slot)

        @pl.when(second_comes)
        def _():
            second(v).wait_recv() if v < vecs - 1 else relay().wait_recv()
            admit(v, second_slot)
            onward(v).wait_recv()
            admit(v, own_slot)

        for k in range(terms):
            prod[:, k * cols:(k + 1) * cols] = jnp.dot(
                left[k], masked[shift[k] + 2], preferred_element_type=F32
            ).astype(BF16)
        summed = lax.dot_general(prod[...], right[...], ROWS_BY_ROWS, preferred_element_type=F32) * mask[2].astype(F32)
        total[v] = summed
        part[v] = summed.astype(BF16)
        if v == 0:
            @pl.when(last)
            def _():
                pl.semaphore_wait(told, 1)

        for d in PEERS:
            share(v, d).start()

    for v in range(vecs):
        own(v).wait_send()
        pl.when(first_goes)(first(v).wait_send)
        pl.when(second_goes)(second(v).wait_send) if v < vecs - 1 else pl.when(first_goes)(relay().wait_send)
        pl.when(first_comes)(onward(v).wait_send)
        if v < vecs - 1:
            for d in PEERS:
                share(v, d).wait_send()
    for v in range(vecs):
        if v == vecs - 1:
            for d in PEERS:
                share(v, d).wait_send()
        result = total[v, pl.ds(pl.multiple_of(t * piece, piece), piece)]
        for d in PEERS[::-1]:
            share(v, d).wait_recv()
            result = result + landed[v, d - 1].astype(F32)
        out_ref[v] = result.astype(BF16)


def solution(mesh):
    sectors, groups = mesh.shape["sec"], mesh.shape["term"]

    def per_device(wave, left, right, shift, lsize, rsize):
        vecs, rows, cols = wave.shape
        terms = left.shape[0]
        piece = rows // groups
        far = len(PEERS)

        def body(*refs):
            kernel(sectors, groups, *refs)

        dma = pltpu.SemaphoreType.DMA
        return pl.pallas_call(
            body,
            name="sigma",
            out_shape=jax.ShapeDtypeStruct((vecs, piece, cols), BF16),
            in_specs=[pl.BlockSpec(memory_space=pltpu.HBM)] * 6,
            out_specs=pl.BlockSpec(memory_space=pltpu.VMEM),
            scratch_shapes=[
                *[pltpu.VMEM((5, rows, cols), BF16) for _ in range(vecs)],
                pltpu.VMEM((terms, rows, rows), BF16),
                pltpu.VMEM((cols, terms * cols), BF16),
                pltpu.VMEM((rows, terms * cols), BF16),
                pltpu.VMEM((5, rows, cols), BF16),
                pltpu.VMEM((5, rows, cols), BF16),
                pltpu.VMEM((vecs, rows, cols), F32),
                pltpu.VMEM((vecs, rows, cols), BF16),
                pltpu.VMEM((vecs, far, piece, cols), BF16),
                pltpu.SMEM(shift.shape, jnp.int32),
                pltpu.SMEM(lsize.shape, jnp.int32),
                pltpu.SMEM(rsize.shape, jnp.int32),
                dma((4 + vecs + terms,)),
                dma((2, vecs)), dma((2, vecs)),
                dma((vecs,)), dma((vecs,)),
                dma((vecs,)), dma((vecs,)),
                dma((vecs, far)), dma((vecs, far)),
                pltpu.SemaphoreType.REGULAR,
                pltpu.SemaphoreType.REGULAR,
            ],
            compiler_params=pltpu.CompilerParams(
                collective_id=0, has_side_effects=True, vmem_limit_bytes=60 * 2**20
            ),
        )(wave, left, right, shift, lsize, rsize)

    return jax.shard_map(
        per_device,
        mesh=mesh,
        in_specs=(P(None, "sec", None), P("term", "sec", None, None), P("term", "sec", None, None), P("term"), P(), P()),
        out_specs=P(None, ("sec", "term"), None),
        check_vma=False,
    )
```

```python
import jax
import jax.numpy as jnp
from jax import lax
from jax.experimental import pallas as pl
from jax.experimental.pallas import tpu as pltpu
from jax.sharding import PartitionSpec as P

MESH = pl.DeviceIdType.MESH
F32, BF16 = jnp.float32, jnp.bfloat16
ROWS_BY_ROWS = (((1,), (1,)), ((), ()))
LINE = 8
PEERS = (4, 3, 5, 2, 6, 1, 7)


def kernel(
    sectors, groups,
    wave_hbm, left_hbm, right_hbm, shift_hbm, lsize_hbm, rsize_hbm,
    out_ref,
    src0, src1, src2, left, right, prod, masked, mask, total, part, landed, shift, lsize, rsize,
    load_sem, z_send, z_recv, c_send, c_recv, f_send, f_recv, y_send, y_recv, told, near,
):
    vecs, rows, cols = total.shape
    terms = left.shape[0]
    piece = rows // groups
    src = (src0, src1, src2)
    s = lax.axis_index("sec")
    t = lax.axis_index("term")
    core = lax.rem(s, 2)
    twin = s + 1 - 2 * core
    up, down = s + 2, s - 2
    has_up, has_down = up < sectors, down >= 0
    beside = s + 2 * core - 1
    along = has_up.astype(jnp.int32) + has_down.astype(jnp.int32) + jnp.where(core == 1, has_up, has_down).astype(jnp.int32)

    def peer(d):
        return lax.rem(t + d, groups)

    barrier = pltpu.get_barrier_semaphore()
    def greet(sem, place):
        pl.semaphore_signal(sem, inc=1, device_id=place, device_id_type=MESH)

    at = lax.rem(s // 2, LINE)
    last, before = at == LINE - 1, at == LINE - 2
    after = (at == 0) & has_down
    first_up = core == 1
    first_goes = jnp.where(first_up, has_up, has_down)

    first_to = jnp.where(core == 1, up, down)
    first_slot = 4 * (1 - core)
    second_to = jnp.where(core == 1, down, up)
    second_slot = 4 * core
    own_slot = 1 + 2 * core
    onward_slot = 3 - 2 * core
    second_goes = jnp.where(core == 1, has_down, has_up)
    first_comes, second_comes = second_goes, first_goes

    def first(v):
        return pltpu.make_async_remote_copy(
            src_ref=wave_hbm.at[v], dst_ref=src[v].at[first_slot], send_sem=z_send.at[0, v], recv_sem=z_recv.at[0, v],
            device_id=(first_to, t), device_id_type=MESH)

    def second(v):
        return pltpu.make_async_remote_copy(
            src_ref=wave_hbm.at[v], dst_ref=src[v].at[second_slot], send_sem=z_send.at[1, v], recv_sem=z_recv.at[1, v],
            device_id=(second_to, t), device_id_type=MESH)

    def own(v):
        return pltpu.make_async_remote_copy(
            src_ref=wave_hbm.at[v], dst_ref=src[v].at[own_slot], send_sem=c_send.at[v], recv_sem=c_recv.at[v],
            device_id=(twin, t), device_id_type=MESH)

    def onward(v):
        return pltpu.make_async_remote_copy(
            src_ref=src[v].at[first_slot], dst_ref=src[v].at[onward_slot], send_sem=f_send.at[v], recv_sem=f_recv.at[v],
            device_id=(twin, t), device_id_type=MESH)

    def relay():
        v = vecs - 1
        return pltpu.make_async_remote_copy(
            src_ref=src[v].at[onward_slot], dst_ref=src[v].at[first_slot], send_sem=z_send.at[1, v], recv_sem=z_recv.at[1, v],
            device_id=(beside, t), device_id_type=MESH)

    def share(v, d):
        there = pl.multiple_of(peer(d) * piece, piece)
        return pltpu.make_async_remote_copy(
            src_ref=part.at[v, pl.ds(there, piece)], dst_ref=landed.at[v, d - 1], send_sem=y_send.at[v, d - 1], recv_sem=y_recv.at[v, d - 1],
            device_id=(s, peer(d)), device_id_type=MESH)

    @pl.when(last)
    def _():
        @pl.when(has_up)
        def _():
            pl.semaphore_wait(barrier, 1 + core)

            @pl.when(first_up)
            def _():
                for v in range(vecs):
                    first(v).start()

            @pl.when(jnp.logical_not(first_up))
            def _():
                for v in range(vecs - 1):
                    second(v).start()

        greet(barrier, (down, t))
        pl.when(jnp.logical_not(first_up))(lambda: greet(barrier, (beside, t)))

        @pl.when(has_up)
        def _():
            greet(told, (up, t))
            pl.when(first_up)(lambda: greet(told, (beside, t)))

    @pl.when(jnp.logical_not(last))
    def _():
        greet(barrier, (twin, t))
        pl.when(has_down)(lambda: greet(barrier, (down, t)))

        @pl.when(has_up & jnp.logical_not(before))
        def _():
            greet(barrier, (up, t))

        @pl.when(first_goes & jnp.logical_not(before & first_up))
        def _():
            greet(barrier, (beside, t))

        for d in PEERS:
            greet(barrier, (s, peer(d)))
        pl.semaphore_wait(barrier, 1 + along - jnp.where(after, 2 - core, 0) + len(PEERS))

        for v in range(vecs):
            pl.when(first_goes & jnp.logical_not(after & (core == 0)))(first(v).start)
            if v < vecs - 1:
                pl.when(second_goes & jnp.logical_not(after & (core == 1)))(second(v).start)

    @pl.when(before)
    def _():
        greet(near, (up, t))
        pl.when(core == 1)(lambda: greet(near, (beside, t)))

    @pl.when(last)
    def _():
        pl.semaphore_wait(near, 2 - core)

    for v in range(vecs):
        pl.when(last & (core == 0))(first(v).start)
        if v < vecs - 1:
            pl.when(last & (core == 1))(second(v).start)
    for v in range(vecs - 1, -1, -1):
        own(v).start()

    own(vecs - 1).wait_recv()
    pl.when(first_goes & jnp.logical_not(after & (core == 0)))(relay().start)

    loads = [
        pltpu.make_async_copy(lsize_hbm, lsize, load_sem.at[0]),
        pltpu.make_async_copy(rsize_hbm, rsize, load_sem.at[1]),
        pltpu.make_async_copy(shift_hbm, shift, load_sem.at[2]),
        pltpu.make_async_copy(left_hbm.at[:, 0], left, load_sem.at[3]),
    ]
    loads += [pltpu.make_async_copy(wave_hbm.at[v], src[v].at[2], load_sem.at[4 + v]) for v in range(vecs)]
    loads += [
        pltpu.make_async_copy(right_hbm.at[k, 0], right.at[:, pl.ds(k * cols, cols)], load_sem.at[4 + vecs + k])
        for k in range(terms)
    ]
    for load in loads:
        load.start()

    loads[0].wait()
    loads[1].wait()
    row_at = lax.broadcasted_iota(jnp.int32, (rows, cols), 0)
    col_at = lax.broadcasted_iota(jnp.int32, (rows, cols), 1)
    for o in range(5):
        q = s + o - 2
        inside = (q >= 0) & (q < sectors)
        q = jnp.clip(q, 0, sectors - 1)
        limit = jnp.where(inside, lsize[q], 0)
        mask[o] = jnp.where((row_at < limit) & (col_at < rsize[q]), 1.0, 0.0).astype(BF16)
    for load in loads[2:]:
        load.wait()

    @pl.when(after)
    def _():
        pl.semaphore_wait(told, 2 - core)

    for v in range(vecs):
        pl.when(after & (core == 0))(first(v).start)
        if v < vecs - 1:
            pl.when(after & (core == 1))(second(v).start)
    pl.when(after & (core == 0))(relay().start)

    @pl.when(before)
    def _():
        for d in PEERS:
            greet(told, (s, peer(d)))
        pl.semaphore_wait(told, len(PEERS))
        greet(told, (up, t))

    def admit(v, slot):
        masked[slot] = src[v][slot] * mask[slot]

    @pl.when(jnp.logical_not(first_comes))
    def _():
        masked[first_slot] = jnp.zeros((rows, cols), BF16)

    @pl.when(jnp.logical_not(second_comes))
    def _():
        masked[second_slot] = jnp.zeros((rows, cols), BF16)
        masked[own_slot] = jnp.zeros((rows, cols), BF16)

    for v in range(vecs):
        admit(v, 2)
        @pl.when(first_comes)
        def _():
            first(v).wait_recv()
            onward(v).start()

        if v < vecs - 1:
            own(v).wait_recv()
        admit(v, onward_slot)

        @pl.when(first_comes)
        def _():
            admit(v, first_slot)

        @pl.when(second_comes)
        def _():
            second(v).wait_recv() if v < vecs - 1 else relay().wait_recv()
            admit(v, second_slot)
            onward(v).wait_recv()
            admit(v, own_slot)

        for k in range(terms):
            prod[:, k * cols:(k + 1) * cols] = jnp.dot(
                left[k], masked[shift[k] + 2], preferred_element_type=F32
            ).astype(BF16)
        summed = lax.dot_general(prod[...], right[...], ROWS_BY_ROWS, preferred_element_type=F32) * mask[2].astype(F32)
        total[v] = summed
        part[v] = summed.astype(BF16)
        if v == 0:
            @pl.when(last)
            def _():
                pl.semaphore_wait(told, 1)

        for d in PEERS:
            share(v, d).start()

    for v in range(vecs):
        own(v).wait_send()
        pl.when(first_goes)(first(v).wait_send)
        pl.when(second_goes)(second(v).wait_send) if v < vecs - 1 else pl.when(first_goes)(relay().wait_send)
        pl.when(first_comes)(onward(v).wait_send)
        if v < vecs - 1:
            for d in PEERS:
                share(v, d).wait_send()
    for v in range(vecs):
        if v == vecs - 1:
            for d in PEERS:
                share(v, d).wait_send()
        result = total[v, pl.ds(pl.multiple_of(t * piece, piece), piece)]
        for d in PEERS[::-1]:
            share(v, d).wait_recv()
            result = result + landed[v, d - 1].astype(F32)
        out_ref[v] = result.astype(BF16)


def solution(mesh):
    sectors, groups = mesh.shape["sec"], mesh.shape["term"]

    def per_device(wave, left, right, shift, lsize, rsize):
        vecs, rows, cols = wave.shape
        terms = left.shape[0]
        piece = rows // groups
        far = len(PEERS)

        def body(*refs):
            kernel(sectors, groups, *refs)

        dma = pltpu.SemaphoreType.DMA
        return pl.pallas_call(
            body,
            name="sigma",
            out_shape=jax.ShapeDtypeStruct((vecs, piece, cols), BF16),
            in_specs=[pl.BlockSpec(memory_space=pltpu.HBM)] * 6,
            out_specs=pl.BlockSpec(memory_space=pltpu.VMEM),
            scratch_shapes=[
                *[pltpu.VMEM((5, rows, cols), BF16) for _ in range(vecs)],
                pltpu.VMEM((terms, rows, rows), BF16),
                pltpu.VMEM((cols, terms * cols), BF16),
                pltpu.VMEM((rows, terms * cols), BF16),
                pltpu.VMEM((5, rows, cols), BF16),
                pltpu.VMEM((5, rows, cols), BF16),
                pltpu.VMEM((vecs, rows, cols), F32),
                pltpu.VMEM((vecs, rows, cols), BF16),
                pltpu.VMEM((vecs, far, piece, cols), BF16),
                pltpu.SMEM(shift.shape, jnp.int32),
                pltpu.SMEM(lsize.shape, jnp.int32),
                pltpu.SMEM(rsize.shape, jnp.int32),
                dma((4 + vecs + terms,)),
                dma((2, vecs)), dma((2, vecs)),
                dma((vecs,)), dma((vecs,)),
                dma((vecs,)), dma((vecs,)),
                dma((vecs, far)), dma((vecs, far)),
                pltpu.SemaphoreType.REGULAR,
                pltpu.SemaphoreType.REGULAR,
            ],
            compiler_params=pltpu.CompilerParams(
                collective_id=0, has_side_effects=True, vmem_limit_bytes=48 * 2**20
            ),
        )(*[pltpu.with_memory_space_constraint(x, pltpu.HBM) for x in (wave, left, right, shift, lsize, rsize)])

    return jax.shard_map(
        per_device,
        mesh=mesh,
        in_specs=(P(None, "sec", None), P("term", "sec", None, None), P("term", "sec", None, None), P("term"), P(), P()),
        out_specs=P(None, ("sec", "term"), None),
        check_vma=False,
    )
```

```python
import jax
import jax.numpy as jnp
from jax import lax
from jax.experimental import pallas as pl
from jax.experimental.pallas import tpu as pltpu
from jax.sharding import PartitionSpec as P

MESH = pl.DeviceIdType.MESH
F32, BF16 = jnp.float32, jnp.bfloat16
ROWS_BY_ROWS = (((1,), (1,)), ((), ()))
LINE = 8
PEERS = (4, 3, 5, 2, 6, 1, 7)


def kernel(
    sectors, groups,
    wave_hbm, left_hbm, right_hbm, shift_hbm, lsize_hbm, rsize_hbm,
    out_ref,
    src0, src1, src2, left, right, prod, masked, mask, total, part, landed, shift, lsize, rsize,
    load_sem, z_send, z_recv, c_send, c_recv, f_send, f_recv, y_send, y_recv, told, near,
):
    vecs, rows, cols = total.shape
    terms = left.shape[0]
    piece = rows // groups
    src = (src0, src1, src2)
    s = lax.axis_index("sec")
    t = lax.axis_index("term")
    core = lax.rem(s, 2)
    twin = s + 1 - 2 * core
    up, down = s + 2, s - 2
    has_up, has_down = up < sectors, down >= 0
    beside = s + 2 * core - 1
    along = has_up.astype(jnp.int32) + has_down.astype(jnp.int32) + jnp.where(core == 1, has_up, has_down).astype(jnp.int32)

    def peer(d):
        return lax.rem(t + d, groups)

    barrier = pltpu.get_barrier_semaphore()
    def greet(sem, place):
        pl.semaphore_signal(sem, inc=1, device_id=place, device_id_type=MESH)

    at = lax.rem(s // 2, LINE)
    last, before = at == LINE - 1, at == LINE - 2
    after = (at == 0) & has_down
    first_up = core == 1
    first_goes = jnp.where(first_up, has_up, has_down)

    first_to = jnp.where(core == 1, up, down)
    first_slot = 4 * (1 - core)
    second_to = jnp.where(core == 1, down, up)
    second_slot = 4 * core
    own_slot = 1 + 2 * core
    onward_slot = 3 - 2 * core
    second_goes = jnp.where(core == 1, has_down, has_up)
    first_comes, second_comes = second_goes, first_goes

    def first(v):
        return pltpu.make_async_remote_copy(
            src_ref=wave_hbm.at[v], dst_ref=src[v].at[first_slot], send_sem=z_send.at[0, v], recv_sem=z_recv.at[0, v],
            device_id=(first_to, t), device_id_type=MESH)

    def second(v):
        return pltpu.make_async_remote_copy(
            src_ref=wave_hbm.at[v], dst_ref=src[v].at[second_slot], send_sem=z_send.at[1, v], recv_sem=z_recv.at[1, v],
            device_id=(second_to, t), device_id_type=MESH)

    def own(v):
        return pltpu.make_async_remote_copy(
            src_ref=wave_hbm.at[v], dst_ref=src[v].at[own_slot], send_sem=c_send.at[v], recv_sem=c_recv.at[v],
            device_id=(twin, t), device_id_type=MESH)

    def onward(v):
        return pltpu.make_async_remote_copy(
            src_ref=src[v].at[first_slot], dst_ref=src[v].at[onward_slot], send_sem=f_send.at[v], recv_sem=f_recv.at[v],
            device_id=(twin, t), device_id_type=MESH)

    def relay():
        v = vecs - 1
        return pltpu.make_async_remote_copy(
            src_ref=src[v].at[onward_slot], dst_ref=src[v].at[first_slot], send_sem=z_send.at[1, v], recv_sem=z_recv.at[1, v],
            device_id=(beside, t), device_id_type=MESH)

    def share(v, d):
        there = pl.multiple_of(peer(d) * piece, piece)
        return pltpu.make_async_remote_copy(
            src_ref=part.at[v, pl.ds(there, piece)], dst_ref=landed.at[v, d - 1], send_sem=y_send.at[v, d - 1], recv_sem=y_recv.at[v, d - 1],
            device_id=(s, peer(d)), device_id_type=MESH)

    @pl.when(last)
    def _():
        @pl.when(has_up)
        def _():
            pl.semaphore_wait(barrier, 1 + core)

            @pl.when(first_up)
            def _():
                for v in range(vecs):
                    first(v).start()

            @pl.when(jnp.logical_not(first_up))
            def _():
                for v in range(vecs - 1):
                    second(v).start()

        greet(barrier, (down, t))
        pl.when(jnp.logical_not(first_up))(lambda: greet(barrier, (beside, t)))

        @pl.when(has_up)
        def _():
            greet(told, (up, t))
            pl.when(first_up)(lambda: greet(told, (beside, t)))

    @pl.when(jnp.logical_not(last))
    def _():
        greet(barrier, (twin, t))
        pl.when(has_down)(lambda: greet(barrier, (down, t)))

        @pl.when(has_up & jnp.logical_not(before))
        def _():
            greet(barrier, (up, t))

        @pl.when(first_goes & jnp.logical_not(before & first_up))
        def _():
            greet(barrier, (beside, t))

        for d in PEERS:
            greet(barrier, (s, peer(d)))
        pl.semaphore_wait(barrier, 1 + along - jnp.where(after, 2 - core, 0) + len(PEERS))

        for v in range(vecs):
            pl.when(first_goes & jnp.logical_not(after & (core == 0)))(first(v).start)
            if v < vecs - 1:
                pl.when(second_goes & jnp.logical_not(after & (core == 1)))(second(v).start)

    @pl.when(before)
    def _():
        greet(near, (up, t))
        pl.when(core == 1)(lambda: greet(near, (beside, t)))

    @pl.when(last)
    def _():
        pl.semaphore_wait(near, 2 - core)

    for v in range(vecs):
        pl.when(last & (core == 0))(first(v).start)
        if v < vecs - 1:
            pl.when(last & (core == 1))(second(v).start)
    for v in range(vecs - 1, -1, -1):
        own(v).start()

    own(vecs - 1).wait_recv()
    pl.when(first_goes & jnp.logical_not(after & (core == 0)))(relay().start)

    loads = [
        pltpu.make_async_copy(lsize_hbm, lsize, load_sem.at[0]),
        pltpu.make_async_copy(rsize_hbm, rsize, load_sem.at[1]),
        pltpu.make_async_copy(shift_hbm, shift, load_sem.at[2]),
        pltpu.make_async_copy(left_hbm.at[:, 0], left, load_sem.at[3]),
    ]
    loads += [pltpu.make_async_copy(wave_hbm.at[v], src[v].at[2], load_sem.at[4 + v]) for v in range(vecs)]
    loads += [
        pltpu.make_async_copy(right_hbm.at[k, 0], right.at[:, pl.ds(k * cols, cols)], load_sem.at[4 + vecs + k])
        for k in range(terms)
    ]
    for load in loads:
        load.start()

    loads[0].wait()
    loads[1].wait()
    row_at = lax.broadcasted_iota(jnp.int32, (rows, cols), 0)
    col_at = lax.broadcasted_iota(jnp.int32, (rows, cols), 1)
    for o in range(5):
        q = s + o - 2
        inside = (q >= 0) & (q < sectors)
        q = jnp.clip(q, 0, sectors - 1)
        limit = jnp.where(inside, lsize[q], 0)
        mask[o] = jnp.where((row_at < limit) & (col_at < rsize[q]), 1.0, 0.0).astype(BF16)
    for load in loads[2:]:
        load.wait()

    row_ok = jnp.where(row_at < lsize[s], 1.0, 0.0).astype(BF16)
    col_ok = jnp.where(row_at < rsize[s], 1.0, 0.0).astype(BF16)
    for k in range(terms):
        left[k] = left[k] * row_ok
        right[:, k * cols:(k + 1) * cols] = right[:, k * cols:(k + 1) * cols] * col_ok

    @pl.when(after)
    def _():
        pl.semaphore_wait(told, 2 - core)

    for v in range(vecs):
        pl.when(after & (core == 0))(first(v).start)
        if v < vecs - 1:
            pl.when(after & (core == 1))(second(v).start)
    pl.when(after & (core == 0))(relay().start)

    @pl.when(before)
    def _():
        for d in PEERS:
            greet(told, (s, peer(d)))
        pl.semaphore_wait(told, len(PEERS))
        greet(told, (up, t))

    def admit(v, slot):
        masked[slot] = src[v][slot] * mask[slot]

    @pl.when(jnp.logical_not(first_comes))
    def _():
        masked[first_slot] = jnp.zeros((rows, cols), BF16)

    @pl.when(jnp.logical_not(second_comes))
    def _():
        masked[second_slot] = jnp.zeros((rows, cols), BF16)
        masked[own_slot] = jnp.zeros((rows, cols), BF16)

    for v in range(vecs):
        admit(v, 2)
        @pl.when(first_comes)
        def _():
            first(v).wait_recv()
            onward(v).start()

        if v < vecs - 1:
            own(v).wait_recv()
        admit(v, onward_slot)

        @pl.when(first_comes)
        def _():
            admit(v, first_slot)

        @pl.when(second_comes)
        def _():
            second(v).wait_recv() if v < vecs - 1 else relay().wait_recv()
            admit(v, second_slot)
            onward(v).wait_recv()
            admit(v, own_slot)

        for k in range(terms):
            prod[:, k * cols:(k + 1) * cols] = jnp.dot(
                left[k], masked[shift[k] + 2], preferred_element_type=F32
            ).astype(BF16)
        summed = lax.dot_general(prod[...], right[...], ROWS_BY_ROWS, preferred_element_type=F32)
        total[v] = summed
        part[v] = summed.astype(BF16)
        if v == 0:
            @pl.when(last)
            def _():
                pl.semaphore_wait(told, 1)

        for d in PEERS:
            share(v, d).start()

    for v in range(vecs):
        own(v).wait_send()
        pl.when(first_goes)(first(v).wait_send)
        pl.when(second_goes)(second(v).wait_send) if v < vecs - 1 else pl.when(first_goes)(relay().wait_send)
        pl.when(first_comes)(onward(v).wait_send)
        if v < vecs - 1:
            for d in PEERS:
                share(v, d).wait_send()
    for v in range(vecs):
        if v == vecs - 1:
            for d in PEERS:
                share(v, d).wait_send()
        result = total[v, pl.ds(pl.multiple_of(t * piece, piece), piece)]
        for d in PEERS[::-1]:
            share(v, d).wait_recv()
            result = result + landed[v, d - 1].astype(F32)
        out_ref[v] = result.astype(BF16)


def solution(mesh):
    sectors, groups = mesh.shape["sec"], mesh.shape["term"]

    def per_device(wave, left, right, shift, lsize, rsize):
        vecs, rows, cols = wave.shape
        terms = left.shape[0]
        piece = rows // groups
        far = len(PEERS)

        def body(*refs):
            kernel(sectors, groups, *refs)

        dma = pltpu.SemaphoreType.DMA
        return pl.pallas_call(
            body,
            name="sigma",
            out_shape=jax.ShapeDtypeStruct((vecs, piece, cols), BF16),
            in_specs=[pl.BlockSpec(memory_space=pltpu.HBM)] * 6,
            out_specs=pl.BlockSpec(memory_space=pltpu.VMEM),
            scratch_shapes=[
                *[pltpu.VMEM((5, rows, cols), BF16) for _ in range(vecs)],
                pltpu.VMEM((terms, rows, rows), BF16),
                pltpu.VMEM((cols, terms * cols), BF16),
                pltpu.VMEM((rows, terms * cols), BF16),
                pltpu.VMEM((5, rows, cols), BF16),
                pltpu.VMEM((5, rows, cols), BF16),
                pltpu.VMEM((vecs, rows, cols), F32),
                pltpu.VMEM((vecs, rows, cols), BF16),
                pltpu.VMEM((vecs, far, piece, cols), BF16),
                pltpu.SMEM(shift.shape, jnp.int32),
                pltpu.SMEM(lsize.shape, jnp.int32),
                pltpu.SMEM(rsize.shape, jnp.int32),
                dma((4 + vecs + terms,)),
                dma((2, vecs)), dma((2, vecs)),
                dma((vecs,)), dma((vecs,)),
                dma((vecs,)), dma((vecs,)),
                dma((vecs, far)), dma((vecs, far)),
                pltpu.SemaphoreType.REGULAR,
                pltpu.SemaphoreType.REGULAR,
            ],
            compiler_params=pltpu.CompilerParams(
                collective_id=0, has_side_effects=True, vmem_limit_bytes=48 * 2**20
            ),
        )(*[pltpu.with_memory_space_constraint(x, pltpu.HBM) for x in (wave, left, right, shift, lsize, rsize)])

    return jax.shard_map(
        per_device,
        mesh=mesh,
        in_specs=(P(None, "sec", None), P("term", "sec", None, None), P("term", "sec", None, None), P("term"), P(), P()),
        out_specs=P(None, ("sec", "term"), None),
        check_vma=False,
    )
```
